128 devices in a mesh: row: 16 (over z_hi, x, core), tm: 8 (over z_lo, y).
Axes of the slice: x: 4, y: 4, z: 4 (z_hi: 2, z_lo: 2; z = z_hi * 2 + z_lo), core: 2. Of those that a mesh axis runs over, the one named last changes fastest.
Arguments:
- snapshots: bfloat16 [8192, 163840], P('tm', 'row'), may hold values from -9 to 9
Outputs:
- lag_gram: float32 [8192, 1123], P(('tm', 'row'))
The draws below stay inside these ranges and needn't reach their ends.
All inputs are finite; a program needn't handle non-finite values.
Results may differ from the reference program's by a relative error of at most 0.0003.
Values may be sent and summed in bfloat16 or wider, within the bound.
A program may use at most 128 MiB of HBM per device.

```python
import math
import jax
import jax.numpy as jnp
from jax import lax

SNAP = 1024
LAG = 100
LAGW = 1123
NT = 8192
RT = 163840
N_TM = 8


def draw_snapshots(key, part):
    key = jax.random.fold_in(key, 11)
    keys = jax.random.split(key, 5)
    times = jnp.arange(NT, dtype=jnp.float32)[:, None]
    place = (jnp.arange(RT, dtype=jnp.float32) + 0.5) * (1.0 / RT)
    rate = (0.15 + 1.7 * place) * jax.random.uniform(keys[0], (RT,), jnp.float32, 0.8, 1.2)
    omega = rate * (math.pi / LAG)
    phase = jax.random.uniform(keys[1], (RT,), jnp.float32, -math.pi, math.pi)
    stamp = jnp.exp(jax.random.uniform(keys[3], (NT, 1), jnp.float32, math.log(0.5), math.log(2.0)))
    jitter = jnp.exp(jax.random.uniform(keys[2], (RT,), jnp.float32, math.log(0.75), math.log(1.33)))
    profile = 0.5 * jnp.exp(math.log(3.0) * place)
    noise = 0.4 * profile * jnp.clip(jax.random.normal(keys[4], (NT, RT), jnp.float32), -3.0, 3.0)
    amplitude = profile * jitter
    wave = amplitude * 1.41421356 * jnp.cos(omega * times + phase)
    return jnp.clip(stamp * (wave + noise), -9.0, 9.0).astype(jnp.bfloat16)


def setup_inputs(seed: int = 0) -> dict:
    arg_keys = jax.random.split(jax.random.key(seed), 2)
    snapshots = draw_snapshots(jax.random.fold_in(arg_keys[1], 71), 0)
    return dict(snapshots=snapshots)


def reference(snapshots):
    tail = jnp.zeros((LAG - 1, snapshots.shape[1]), jnp.bfloat16)
    padded = jnp.concatenate([snapshots, tail], axis=0)

    def one_block(index):
        start = (index * SNAP).astype(jnp.int32)
        rows = lax.dynamic_slice_in_dim(padded, start, SNAP, 0)
        reach = lax.dynamic_slice_in_dim(padded, start, LAGW, 0)
        return jnp.dot(rows, reach.T, preferred_element_type=jnp.float32)

    blocks = lax.map(one_block, jnp.arange(N_TM, dtype=jnp.int32))
    return blocks.reshape(NT, LAGW) * (1.0 / RT)
```

```python
import functools

import jax
import jax.numpy as jnp
from jax import lax
from jax.experimental import pallas as pl
from jax.experimental.pallas import tpu as pltpu
from jax.sharding import PartitionSpec as P

MESH = pl.DeviceIdType.MESH
LAG = 100
CHIPS = 8
TM = 8
TILE = 256
BULK = 96
REST = LAG - 1 - BULK
PIECES = 5
SLOT = 128
CHUNKS = 20
NT = (((1,), (1,)), ((), ()))


def outer(left, right):
    return lax.dot_general(left, right, NT, preferred_element_type=jnp.float32)


def kernel(
    a_ref,
    out_ref,
    a_v,
    tail_v,
    packed_src,
    packed_dst,
    strip,
    acc,
    acc_s,
    pair,
    pair_s,
    part,
    part_s,
    got,
    got_s,
    load_sem,
    tail_sem,
    strip_send,
    strip_recv,
    packed_sem,
    pair_send,
    pair_recv,
    got_send,
    got_recv,
):
    depth = a_v.shape[1]
    groups = acc.shape[0]
    row, tm = lax.axis_index("row"), lax.axis_index("tm")
    chip, core = row // 2, row % 2
    partner = (chip * 2 + 1 - core, tm)
    before = (row, (tm + TM - 1) % TM)
    after = (row, (tm + 1) % TM)

    def peer(other):
        return (other * 2 + core, tm)

    tail = pltpu.make_async_copy(a_ref.at[pl.ds(BULK, 16)], tail_v, tail_sem)
    tail.start()

    def load(block):
        rows = pl.ds(block * TILE, TILE)
        return pltpu.make_async_copy(a_ref.at[rows], a_v.at[rows], load_sem.at[block])

    for block in range(groups):
        load(block).start()

    barrier = pltpu.get_barrier_semaphore()
    pl.semaphore_signal(barrier, inc=1, device_id=partner, device_id_type=MESH)
    for d in range(1, CHIPS):
        pl.semaphore_signal(
            barrier, inc=1, device_id=peer((chip + d) % CHIPS), device_id_type=MESH
        )

    @pl.when(tm > 0)
    def _():
        pl.semaphore_signal(barrier, inc=1, device_id=before, device_id_type=MESH)

    @pl.when(tm < TM - 1)
    def _():
        pl.semaphore_signal(barrier, inc=1, device_id=after, device_id_type=MESH)

    tail.wait()
    piece = depth // PIECES
    rows16 = lax.broadcasted_iota(jnp.int32, (16, piece), 0)
    packed = jnp.zeros((16, piece), jnp.float32)
    for p in range(PIECES):
        x = tail_v[:, p * piece : (p + 1) * piece].astype(jnp.float32)
        x = jnp.where(rows16 < REST, x, 0.0)
        packed += x if p == 0 else pltpu.roll(x, REST * p, 0)
    packed_src[...] = packed.astype(jnp.bfloat16)

    inner = (tm > 0).astype(jnp.int32) + (tm < TM - 1).astype(jnp.int32)
    pl.semaphore_wait(barrier, CHIPS + inner)

    width = depth // CHUNKS

    def send_strip(i):
        cols = pl.ds(pl.multiple_of(i * width, width), width)
        return pltpu.make_async_remote_copy(
            src_ref=a_ref.at[pl.ds(0, BULK), cols],
            dst_ref=strip.at[pl.ds(0, BULK), cols],
            send_sem=strip_send.at[i],
            recv_sem=strip_recv.at[i],
            device_id=before,
            device_id_type=MESH,
        )

    send_packed = pltpu.make_async_remote_copy(
        src_ref=packed_src,
        dst_ref=packed_dst,
        send_sem=packed_sem.at[0],
        recv_sem=packed_sem.at[1],
        device_id=before,
        device_id_type=MESH,
    )

    @pl.when(tm > 0)
    def _():
        send_packed.start()

        def go(i, _):
            send_strip(i).start()
            return 0

        lax.fori_loop(0, CHUNKS, go, 0)

    acc_s[...] = jnp.zeros_like(acc_s)
    strip[pl.ds(112, 16), :] = jnp.zeros((16, depth), jnp.bfloat16)

    def to_pair(g, src, dst):
        return pltpu.make_async_remote_copy(
            src_ref=src.at[:, 1 - core],
            dst_ref=dst,
            send_sem=pair_send.at[g],
            recv_sem=pair_recv.at[g],
            device_id=partner,
            device_id_type=MESH,
        )

    def pair_of(g):
        return to_pair(g, acc.at[g], pair.at[g])

    def to_chip(g, src, dst, d):
        other = (chip + d) % CHIPS
        return pltpu.make_async_remote_copy(
            src_ref=src.at[other],
            dst_ref=dst.at[chip],
            send_sem=got_send.at[g, d],
            recv_sem=got_recv.at[g, d],
            device_id=peer(other),
            device_id_type=MESH,
        )

    def exchange(g, total, from_pair, src, dst, copy):
        copy.wait_recv()
        for q in range(CHIPS):
            src[q] = total[q, core] + from_pair[q]
        for d in range(1, CHIPS):
            to_chip(g, src, dst, d).start()

    def collect(g, src, dst, cols):
        total = src[chip]
        for d in range(1, CHIPS):
            to_chip(g, src, dst, d).wait_recv()
            total += dst[(chip + CHIPS - d) % CHIPS]
        out_ref[:, cols] = total

    def exchange_group(g):
        exchange(g, acc.at[g], pair.at[g], part.at[g], got.at[g], pair_of(g))

    def collect_group(g):
        collect(g, part.at[g], got.at[g], pl.ds(g * TILE, TILE))

    own = TILE // 128
    for block in range(groups):
        load(block).wait()
        rows = pl.ds(block * TILE, TILE)
        tile = outer(a_v[rows, :], a_v[pl.ds(0, TILE), :])
        acc[0, pl.ds(block * own, own)] = tile.reshape(own, 2, 64, TILE)
    pair_of(0).start()
    for g in range(1, groups):
        tile = outer(a_v[...], a_v[pl.ds(g * TILE, TILE), :])
        acc[g] = tile.reshape(CHIPS, 2, 64, TILE)
        pair_of(g).start()
        exchange_group(g - 1)

    def strip_chunk(i):
        cols = pl.ds(pl.multiple_of(i * width, width), width)
        send_strip(i).wait_recv()
        tile = outer(a_v[:, cols], strip[:, cols])
        acc_s[...] += tile.reshape(CHIPS, 2, 64, SLOT)

    @pl.when(tm < TM - 1)
    def _():
        send_packed.wait_recv()
        packed = packed_dst[...].astype(jnp.float32)
        for p in range(PIECES):
            x = packed if p == 0 else pltpu.roll(packed, 16 - REST * p, 0)
            x = jnp.where(rows16 < REST, x, 0.0)
            strip[pl.ds(BULK, 16), pl.ds(p * piece, piece)] = x.astype(jnp.bfloat16)

        strip_chunk(0)

    exchange_group(groups - 1)

    @pl.when(tm < TM - 1)
    def _():
        def early(i, _):
            strip_chunk(i)
            return 0

        lax.fori_loop(1, CHUNKS // 2, early, 0)

    for g in range(groups - 1):
        collect_group(g)

    @pl.when(tm < TM - 1)
    def _():
        def late(i, _):
            strip_chunk(i)
            return 0

        lax.fori_loop(CHUNKS // 2, CHUNKS, late, 0)

    pair_s_copy = to_pair(groups, acc_s, pair_s)
    pair_s_copy.start()
    collect_group(groups - 1)
    exchange(groups, acc_s, pair_s, part_s, got_s, pair_s_copy)
    collect(groups, part_s, got_s, pl.ds(groups * TILE, SLOT))

    @pl.when(tm > 0)
    def _():
        send_packed.wait_send()

        def done(i, _):
            send_strip(i).wait_send()
            return 0

        lax.fori_loop(0, CHUNKS, done, 0)

    for g in range(groups):
        pair_of(g).wait_send()
    pair_s_copy.wait_send()
    for d in range(1, CHIPS):
        for g in range(groups):
            to_chip(g, part.at[g], got.at[g], d).wait_send()
        to_chip(groups, part_s, got_s, d).wait_send()


def on_device(snapshots):
    snap, depth = snapshots.shape
    groups = snap // TILE
    mine = snap // lax.axis_size("row")
    total_rows = depth * lax.axis_size("row")
    columns = snap + LAG - 1
    f32, bf16 = jnp.float32, jnp.bfloat16
    dma = pltpu.SemaphoreType.DMA
    summed = pl.pallas_call(
        kernel,
        out_shape=jax.ShapeDtypeStruct((mine, snap + SLOT), f32),
        in_specs=[pl.BlockSpec(memory_space=pl.ANY)],
        out_specs=pl.BlockSpec(memory_space=pltpu.VMEM),
        scratch_shapes=[
            pltpu.VMEM((snap, depth), bf16),
            pltpu.VMEM((16, depth), bf16),
            pltpu.VMEM((16, depth // PIECES), bf16),
            pltpu.VMEM((16, depth // PIECES), bf16),
            pltpu.VMEM((SLOT, depth), bf16),
            pltpu.VMEM((groups, CHIPS, 2, mine, TILE), f32),
            pltpu.VMEM((CHIPS, 2, mine, SLOT), f32),
            pltpu.VMEM((groups, CHIPS, mine, TILE), f32),
            pltpu.VMEM((CHIPS, mine, SLOT), f32),
            pltpu.VMEM((groups, CHIPS, mine, TILE), f32),
            pltpu.VMEM((CHIPS, mine, SLOT), f32),
            pltpu.VMEM((groups, CHIPS, mine, TILE), f32),
            pltpu.VMEM((CHIPS, mine, SLOT), f32),
            dma((groups,)),
            dma,
            dma((CHUNKS,)),
            dma((CHUNKS,)),
            dma((2,)),
            dma((groups + 1,)),
            dma((groups + 1,)),
            dma((groups + 1, CHIPS)),
            dma((groups + 1, CHIPS)),
        ],
        compiler_params=pltpu.CompilerParams(
            collective_id=0, has_side_effects=True, vmem_limit_bytes=56 * 2**20
        ),
        name="lagged_gram",
    )(snapshots)
    return summed[:, :columns] * (1.0 / total_rows)


def solution(mesh):
    return jax.shard_map(
        on_device,
        mesh=mesh,
        in_specs=(P("tm", "row"),),
        out_specs=P(("tm", "row"), None),
        check_vma=False,
    )
```

```python
import jax
import jax.numpy as jnp
from jax import lax
from jax.experimental import pallas as pl
from jax.experimental.pallas import tpu as pltpu
from jax.sharding import PartitionSpec as P

MESH = pl.DeviceIdType.MESH
LAG = 100
CHIPS = 8
TM = 8
TILE = 256
GROUPS = 4
BULK = 96
REST = LAG - 1 - BULK
PIECES = 5
SLOT = 128
CHUNKS = 20
LONG = 5
HALF = CHUNKS // 2
NEAR = CHUNKS - LONG
NT = (((1,), (1,)), ((), ()))


def outer(left, right):
    return lax.dot_general(left, right, NT, preferred_element_type=jnp.float32)


def loop(start, stop, body):
    def step(i, carry):
        body(i)
        return carry

    lax.fori_loop(start, stop, step, 0)


def kernel(
    a_ref,
    out_ref,
    a_v,
    tail_v,
    packed_src,
    packed_dst,
    strip,
    first,
    second,
    via,
    acc,
    acc_s,
    pair,
    pair_s,
    part,
    part_s,
    got_x,
    mid,
    got_z,
    got_s,
    load_sem,
    tail_sem,
    strip_send,
    strip_recv,
    packed_sem,
    first_sem,
    second_sem,
    third_send,
    via_sem,
    away_send,
    pair_sem,
    x_sem,
    z_sem,
    s_sem,
):
    depth = a_v.shape[1]
    row, tm = lax.axis_index("row"), lax.axis_index("tm")
    chip, core = row // 2, row % 2
    zh, x = chip // 4, chip % 4
    zl, y = tm // 4, tm % 4
    partner = (chip * 2 + 1 - core, tm)
    before = (row, (tm + TM - 1) % TM)
    up = (row, zl * 4 + (y + 1) % 4)
    down = (row, zl * 4 + (y + 3) % 4)

    def peer(other):
        return (other * 2 + core, tm)

    def remote(src, dst, send, recv, device):
        return pltpu.make_async_remote_copy(
            src_ref=src,
            dst_ref=dst,
            send_sem=send,
            recv_sem=recv,
            device_id=device,
            device_id_type=MESH,
        )

    tail = pltpu.make_async_copy(a_ref.at[pl.ds(BULK, 16)], tail_v, tail_sem)
    tail.start()

    def load(block):
        rows = pl.ds(pl.multiple_of(block * TILE, TILE), TILE)
        return pltpu.make_async_copy(a_ref.at[rows], a_v.at[rows], load_sem.at[block])

    loop(0, GROUPS, lambda block: load(block).start())

    barrier = pltpu.get_barrier_semaphore()

    def greet(device):
        pl.semaphore_signal(barrier, inc=1, device_id=device, device_id_type=MESH)

    greet(up)
    greet(down)
    greet(partner)
    for d in range(1, CHIPS):
        greet(peer((chip + d) % CHIPS))

    @pl.when(tm == 0)
    def _():
        greet((row, 4))

    @pl.when(tm == 3)
    def _():
        greet((row, 4))

    @pl.when(tm == 4)
    def _():
        greet((row, 0))
        greet((row, 3))

    tail.wait()
    piece = depth // PIECES
    rows16 = lax.broadcasted_iota(jnp.int32, (16, piece), 0)
    packed = jnp.zeros((16, piece), jnp.float32)
    for p in range(PIECES):
        part_p = tail_v[:, p * piece : (p + 1) * piece].astype(jnp.float32)
        part_p = jnp.where(rows16 < REST, part_p, 0.0)
        packed += part_p if p == 0 else pltpu.roll(part_p, REST * p, 0)
    packed_src[...] = packed.astype(jnp.bfloat16)

    more = (tm == 0).astype(jnp.int32) + (tm == 3).astype(jnp.int32)
    more = more + 2 * (tm == 4).astype(jnp.int32)
    pl.semaphore_wait(barrier, CHIPS + 2 + more)

    width = depth // CHUNKS

    def cols(i):
        return pl.ds(pl.multiple_of(i * width, width), width)

    def source(i):
        return a_ref.at[pl.ds(0, BULK), cols(i)]

    def landing(i):
        return strip.at[pl.ds(0, BULK), cols(i)]

    def near(i):
        return remote(source(i), landing(i), strip_send.at[i], strip_recv.at[i], before)

    def hop1(k):
        dst = first.at[:, cols(k)]
        return remote(source(NEAR + k), dst, first_sem.at[0, k], first_sem.at[1, k], up)

    def hop2(k):
        src, dst = first.at[:, cols(k)], second.at[:, cols(k)]
        return remote(src, dst, second_sem.at[0, k], second_sem.at[1, k], up)

    def hop3(k):
        src, dst = second.at[:, cols(k)], landing(NEAR + k)
        return remote(src, dst, third_send.at[k], strip_recv.at[NEAR + k], up)

    def via1(k):
        dst = via.at[:, cols(k)]
        return remote(source(HALF + k), dst, via_sem.at[0, k], via_sem.at[1, k], (row, 0))

    def via2(k):
        src, dst = via.at[:, cols(k)], landing(HALF + k)
        return remote(src, dst, away_send.at[k], strip_recv.at[HALF + k], (row, 3))

    send_packed = remote(
        packed_src, packed_dst, packed_sem.at[0], packed_sem.at[1], before
    )
    sends1, sends2, sends3 = y != 0, y != 1, y != 2

    @pl.when(tm > 0)
    def _():
        send_packed.start()

    def begin(i):
        @pl.when(tm > 0)
        def _():
            near(i).start()

        @pl.when(sends1 & (i < LONG))
        def _():
            hop1(i).start()

        @pl.when(tm == 4)
        def _():
            via1(i).start()

    def begin_rest(i):
        @pl.when((tm > 0) & (tm != 4))
        def _():
            near(i).start()

    loop(0, HALF, begin)
    loop(HALF, NEAR, begin_rest)

    acc_s[...] = jnp.zeros_like(acc_s)
    strip[pl.ds(112, 16), :] = jnp.zeros((16, depth), jnp.bfloat16)

    def forward(p):
        @pl.when(sends2 & (p < LONG))
        def _():
            hop1(p).wait_recv()
            hop2(p).start()

        @pl.when(sends3 & (p >= LONG))
        def _():
            hop2(p - LONG).wait_recv()
            hop3(p - LONG).start()

        @pl.when(tm == 0)
        def _():
            via1(p).wait_recv()
            via2(p).start()

    def pair_of(g):
        src = acc.at[g, :, 1 - core]
        return remote(src, pair.at[g], pair_sem.at[0, g], pair_sem.at[1, g], partner)

    def x_of(g, d):
        other = (x + d) % 4
        src, dst = part.at[g, :, other], got_x.at[g, d]
        return remote(
            src, dst, x_sem.at[0, g, d], x_sem.at[1, g, d], peer(zh * 4 + other)
        )

    def z_of(g):
        src, dst = mid.at[g, 1 - zh], got_z.at[g]
        return remote(
            src, dst, z_sem.at[0, g], z_sem.at[1, g], peer((1 - zh) * 4 + x)
        )

    def exchange_x(g):
        pair_of(g).wait_recv()
        for q in range(CHIPS):
            part[g, q // 4, q % 4] = acc[g, q, core] + pair[g, q]
        for d in (2, 1, 3):
            x_of(g, d).start()

    def exchange_z(g):
        for d in (1, 3, 2):
            x_of(g, d).wait_recv()
        for half in range(2):
            total = part[g, half, x]
            for d in range(1, 4):
                total += got_x[g, d, half]
            mid[g, half] = total
        z_of(g).start()

    def finish(g):
        z_of(g).wait_recv()
        columns = pl.ds(pl.multiple_of(g * TILE, TILE), TILE)
        out_ref[:, columns] = mid[g, zh] + got_z[g]

    def one_tile(t):
        def past(bound):
            return (t >= bound).astype(jnp.int32)

        left = past(4) + past(7) + past(9)
        low = t - 4 * past(4) - 3 * past(7) - 2 * past(9) + left

        @pl.when(t < GROUPS)
        def _():
            load(t).wait()

        rows = pl.ds(pl.multiple_of(low * TILE, TILE), TILE)
        columns = pl.ds(pl.multiple_of(left * TILE, TILE), TILE)
        tile = outer(a_v[rows, :], a_v[columns, :])
        acc[left, pl.ds(low * 2, 2)] = tile.reshape(2, 2, 64, TILE)
        acc[low, pl.ds(left * 2, 2)] = tile.T.reshape(2, 2, 64, TILE)

        @pl.when(low == GROUPS - 1)
        def _():
            pair_of(left).start()

        @pl.when((t != 0) & (t != 3) & (t != 7))
        def _():
            forward(t - 1 - past(4) - past(8))

        @pl.when((t == 4) | (t == 7) | (t == 9))
        def _():
            exchange_x(past(5) + past(8))

    loop(0, 10, one_tile)

    def strip_chunk(i):
        near(i).wait_recv()
        tile = outer(a_v[:, cols(i)], strip[:, cols(i)])
        acc_s[...] += tile.reshape(CHIPS, 2, 64, SLOT)

    @pl.when(tm < TM - 1)
    def _():
        send_packed.wait_recv()
        packed = packed_dst[...].astype(jnp.float32)
        for p in range(PIECES):
            part_p = packed if p == 0 else pltpu.roll(packed, 16 - REST * p, 0)
            part_p = jnp.where(rows16 < REST, part_p, 0.0)
            strip[pl.ds(BULK, 16), pl.ds(p * piece, piece)] = part_p.astype(
                jnp.bfloat16
            )

    def one_chunk(pos):
        @pl.when(tm < TM - 1)
        def _():
            late = pos - HALF
            chunk = jnp.where(late < 0, pos, HALF + late // 2 + LONG * (late % 2))
            strip_chunk(chunk)

        @pl.when((pos == 0) | (pos == 2) | (pos == 6))
        def _():
            forward(7 + (pos > 1).astype(jnp.int32) + (pos > 5).astype(jnp.int32))

        @pl.when(pos == 1)
        def _():
            exchange_x(GROUPS - 1)

        @pl.when((pos == 3) | (pos == 8) | (pos == 14))
        def _():
            exchange_z((pos > 4).astype(jnp.int32) + (pos > 10).astype(jnp.int32))

    loop(0, CHUNKS, one_chunk)

    def s_pair():
        src = acc_s.at[:, 1 - core]
        return remote(src, pair_s, s_sem.at[0, 0], s_sem.at[1, 0], partner)

    def s_of(d):
        other = (chip + d) % CHIPS
        src, dst = part_s.at[other], got_s.at[d]
        return remote(src, dst, s_sem.at[0, d], s_sem.at[1, d], peer(other))

    s_pair().start()
    exchange_z(GROUPS - 1)
    s_pair().wait_recv()
    for q in range(CHIPS):
        part_s[q] = acc_s[q, core] + pair_s[q]
    for d in range(1, CHIPS):
        s_of(d).start()
    loop(0, GROUPS, finish)
    total = part_s[chip]
    for d in range(1, CHIPS):
        s_of(d).wait_recv()
        total += got_s[d]
    out_ref[:, pl.ds(GROUPS * TILE, SLOT)] = total

    @pl.when(tm > 0)
    def _():
        send_packed.wait_send()

    def ended(i):
        @pl.when((tm > 0) & ((tm != 4) | (i < HALF)))
        def _():
            near(i).wait_send()

    loop(0, NEAR, ended)

    def ended_long(k):
        @pl.when(sends1)
        def _():
            hop1(k).wait_send()

        @pl.when(sends2)
        def _():
            hop2(k).wait_send()

        @pl.when(sends3)
        def _():
            hop3(k).wait_send()

    loop(0, LONG, ended_long)

    def ended_via(k):
        @pl.when(tm == 4)
        def _():
            via1(k).wait_send()

        @pl.when(tm == 0)
        def _():
            via2(k).wait_send()

    loop(0, HALF, ended_via)

    def ended_group(g):
        pair_of(g).wait_send()
        z_of(g).wait_send()
        for d in range(1, 4):
            x_of(g, d).wait_send()

    loop(0, GROUPS, ended_group)
    s_pair().wait_send()
    for d in range(1, CHIPS):
        s_of(d).wait_send()


def on_device(snapshots):
    snap, depth = snapshots.shape
    mine = snap // lax.axis_size("row")
    total_rows = depth * lax.axis_size("row")
    columns = snap + LAG - 1
    width = depth // CHUNKS
    f32, bf16 = jnp.float32, jnp.bfloat16
    dma = pltpu.SemaphoreType.DMA
    summed = pl.pallas_call(
        kernel,
        out_shape=jax.ShapeDtypeStruct((mine, snap + SLOT), f32),
        in_specs=[pl.BlockSpec(memory_space=pl.ANY)],
        out_specs=pl.BlockSpec(memory_space=pltpu.VMEM),
        scratch_shapes=[
            pltpu.VMEM((snap, depth), bf16),
            pltpu.VMEM((16, depth), bf16),
            pltpu.VMEM((16, depth // PIECES), bf16),
            pltpu.VMEM((16, depth // PIECES), bf16),
            pltpu.VMEM((SLOT, depth), bf16),
            pltpu.VMEM((BULK, LONG * width), bf16),
            pltpu.VMEM((BULK, LONG * width), bf16),
            pltpu.VMEM((BULK, HALF * width), bf16),
            pltpu.VMEM((GROUPS, CHIPS, 2, mine, TILE), f32),
            pltpu.VMEM((CHIPS, 2, mine, SLOT), f32),
            pltpu.VMEM((GROUPS, CHIPS, mine, TILE), f32),
            pltpu.VMEM((CHIPS, mine, SLOT), f32),
            pltpu.VMEM((GROUPS, 2, 4, mine, TILE), f32),
            pltpu.VMEM((CHIPS, mine, SLOT), f32),
            pltpu.VMEM((GROUPS, 4, 2, mine, TILE), f32),
            pltpu.VMEM((GROUPS, 2, mine, TILE), f32),
            pltpu.VMEM((GROUPS, mine, TILE), f32),
            pltpu.VMEM((CHIPS, mine, SLOT), f32),
            dma((GROUPS,)),
            dma,
            dma((CHUNKS,)),
            dma((CHUNKS,)),
            dma((2,)),
            dma((2, LONG)),
            dma((2, LONG)),
            dma((LONG,)),
            dma((2, HALF)),
            dma((HALF,)),
            dma((2, GROUPS)),
            dma((2, GROUPS, 4)),
            dma((2, GROUPS)),
            dma((2, CHIPS)),
        ],
        compiler_params=pltpu.CompilerParams(
            collective_id=0, has_side_effects=True, vmem_limit_bytes=56 * 2**20
        ),
        name="lagged_gram",
    )(snapshots)
    return summed[:, :columns] * (1.0 / total_rows)


def solution(mesh):
    return jax.shard_map(
        on_device,
        mesh=mesh,
        in_specs=(P("tm", "row"),),
        out_specs=P(("tm", "row"), None),
        check_vma=False,
    )
```

```python
import jax
import jax.numpy as jnp
from jax import lax
from jax.experimental import pallas as pl
from jax.experimental.pallas import tpu as pltpu
from jax.sharding import PartitionSpec as P

MESH = pl.DeviceIdType.MESH
LAG = 100
CHIPS = 8
TM = 8
TILE = 256
GROUPS = 4
BULK = 96
REST = LAG - 1 - BULK
PIECES = 5
SLOT = 128
CHUNKS = 20
LONG = 5
HALF = CHUNKS // 2
NEAR = CHUNKS - LONG
NT = (((1,), (1,)), ((), ()))


def outer(left, right):
    return lax.dot_general(left, right, NT, preferred_element_type=jnp.float32)


def loop(start, stop, body):
    def step(i, carry):
        body(i)
        return carry

    lax.fori_loop(start, stop, step, 0)


def kernel(
    a_ref,
    out_ref,
    a_v,
    packed_src,
    packed_dst,
    strip,
    first,
    second,
    via,
    acc,
    acc_s,
    pair,
    pair_s,
    part,
    part_s,
    got_x,
    mid,
    got_z,
    mid4,
    got_z4,
    got_s,
    load_sem,
    tail_sem,
    strip_send,
    strip_recv,
    packed_sem,
    first_sem,
    second_sem,
    third_send,
    via_sem,
    away_send,
    pair_sem,
    x_sem,
    z_sem,
    s_sem,
):
    depth = a_v.shape[1]
    row, tm = lax.axis_index("row"), lax.axis_index("tm")
    chip, core = row // 2, row % 2
    zh, x = chip // 4, chip % 4
    zl, y = tm // 4, tm % 4
    partner = (chip * 2 + 1 - core, tm)
    before = (row, (tm + TM - 1) % TM)
    up = (row, zl * 4 + (y + 1) % 4)
    down = (row, zl * 4 + (y + 3) % 4)

    def peer(other):
        return (other * 2 + core, tm)

    def remote(src, dst, send, recv, device):
        return pltpu.make_async_remote_copy(
            src_ref=src,
            dst_ref=dst,
            send_sem=send,
            recv_sem=recv,
            device_id=device,
            device_id_type=MESH,
        )

    def load_rows(start, size, sem):
        rows = pl.ds(start, size)
        return pltpu.make_async_copy(a_ref.at[rows], a_v.at[rows], sem)

    head = load_rows(0, SLOT, tail_sem.at[0])
    rest = load_rows(SLOT, TILE - SLOT, tail_sem.at[1])
    head.start()

    def load(block):
        rows = pl.ds(pl.multiple_of(block * TILE, TILE), TILE)
        return pltpu.make_async_copy(a_ref.at[rows], a_v.at[rows], load_sem.at[block])

    barrier = pltpu.get_barrier_semaphore()

    def greet(device):
        pl.semaphore_signal(barrier, inc=1, device_id=device, device_id_type=MESH)

    greet(up)
    greet(down)
    greet(partner)
    for d in range(1, CHIPS):
        greet(peer((chip + d) % CHIPS))

    @pl.when(tm == 0)
    def _():
        greet((row, 4))

    @pl.when(tm == 3)
    def _():
        greet((row, 4))

    @pl.when(tm == 4)
    def _():
        greet((row, 0))
        greet((row, 3))

    head.wait()
    rest.start()
    loop(1, GROUPS, lambda block: load(block).start())
    more = (tm == 0).astype(jnp.int32) + (tm == 3).astype(jnp.int32)
    more = more + 2 * (tm == 4).astype(jnp.int32)
    pl.semaphore_wait(barrier, CHIPS + 2 + more)

    width = depth // CHUNKS

    def cols(i):
        return pl.ds(pl.multiple_of(i * width, width), width)

    def source(i):
        return a_v.at[pl.ds(0, BULK), cols(i)]

    def landing(i):
        return strip.at[i, pl.ds(0, BULK)]

    def near(i):
        return remote(source(i), landing(i), strip_send.at[i], strip_recv.at[i], before)

    def hop1(k):
        dst = first.at[k]
        return remote(source(NEAR + k), dst, first_sem.at[0, k], first_sem.at[1, k], up)

    def hop2(k):
        src, dst = first.at[k], second.at[k]
        return remote(src, dst, second_sem.at[0, k], second_sem.at[1, k], up)

    def hop3(k):
        src, dst = second.at[k], landing(NEAR + k)
        return remote(src, dst, third_send.at[k], strip_recv.at[NEAR + k], up)

    def via1(k):
        dst = via.at[k]
        return remote(source(HALF + k), dst, via_sem.at[0, k], via_sem.at[1, k], (row, 0))

    def via2(k):
        src, dst = via.at[k], landing(HALF + k)
        return remote(src, dst, away_send.at[k], strip_recv.at[HALF + k], (row, 3))

    send_packed = remote(
        packed_src, packed_dst, packed_sem.at[0], packed_sem.at[1], before
    )
    sends1, sends2, sends3 = y != 0, y != 1, y != 2

    def begin(i):
        @pl.when(tm > 0)
        def _():
            near(i).start()

        @pl.when(sends1 & (i < LONG))
        def _():
            hop1(i).start()

        @pl.when(tm == 4)
        def _():
            via1(i).start()

    def begin_rest(i):
        @pl.when((tm > 0) & (tm != 4))
        def _():
            near(i).start()

    loop(0, 2, begin)

    piece = depth // PIECES
    rows16 = lax.broadcasted_iota(jnp.int32, (16, piece), 0)
    packed = jnp.zeros((16, piece), jnp.float32)
    for p in range(PIECES):
        part_p = a_v[BULK : BULK + 16, p * piece : (p + 1) * piece].astype(jnp.float32)
        part_p = jnp.where(rows16 < REST, part_p, 0.0)
        packed += part_p if p == 0 else pltpu.roll(part_p, REST * p, 0)
    packed_src[...] = packed.astype(jnp.bfloat16)

    @pl.when(tm > 0)
    def _():
        send_packed.start()

    loop(2, HALF, begin)
    loop(HALF, NEAR, begin_rest)

    acc_s[...] = jnp.zeros_like(acc_s)
    strip[:, BULK + 16 :, :] = jnp.zeros(
        (CHUNKS, SLOT - BULK - 16, width), jnp.bfloat16
    )

    def forward(p):
        @pl.when(sends2 & (p < LONG))
        def _():
            hop1(p).wait_recv()
            hop2(p).start()

        @pl.when(sends3 & (p >= LONG))
        def _():
            hop2(p - LONG).wait_recv()
            hop3(p - LONG).start()

        @pl.when(tm == 0)
        def _():
            via1(p).wait_recv()
            via2(p).start()

    def pair_of(g):
        src = acc.at[g, :, 1 - core]
        return remote(src, pair.at[g], pair_sem.at[0, g], pair_sem.at[1, g], partner)

    def x_of(g, d):
        other = (x + d) % 4
        src, dst = part.at[g, :, other], got_x.at[g, d]
        return remote(
            src, dst, x_sem.at[0, g, d], x_sem.at[1, g, d], peer(zh * 4 + other)
        )

    def z_of(g):
        src, dst = mid.at[g, 1 - zh], got_z.at[g]
        return remote(
            src, dst, z_sem.at[0, g], z_sem.at[1, g], peer((1 - zh) * 4 + x)
        )

    last = GROUPS - 1

    def sum_pair(g):
        pair_of(g).wait_recv()
        for q in range(CHIPS):
            part[g, q // 4, q % 4] = acc[g, q, core] + pair[g, q]

    def exchange_x(g):
        sum_pair(g)
        for d in (2, 1, 3):
            x_of(g, d).start()

    def exchange_z(g):
        for d in (1, 3, 2):
            x_of(g, d).wait_recv()
        for half in range(2):
            total = part[g, half, x]
            for d in range(1, 4):
                total += got_x[g, d, half]
            mid[g, half] = total
        z_of(g).start()

    def finish(g):
        z_of(g).wait_recv()
        columns = pl.ds(pl.multiple_of(g * TILE, TILE), TILE)
        out_ref[:, columns] = mid[g, zh] + got_z[g]

    def z_first():
        src = part.at[last, 1 - zh]
        return remote(
            src, got_z4, z_sem.at[0, last], z_sem.at[1, last], peer((1 - zh) * 4 + x)
        )

    def x_last(d):
        other = (x + d) % 4
        return remote(
            mid4.at[other],
            got_x.at[last, d, 0],
            x_sem.at[0, last, d],
            x_sem.at[1, last, d],
            peer(zh * 4 + other),
        )

    def last_z():
        sum_pair(last)
        z_first().start()

    def last_x():
        z_first().wait_recv()
        for q in range(4):
            mid4[q] = part[last, zh, q] + got_z4[q]
        for d in (2, 1, 3):
            x_last(d).start()

    def last_finish():
        total = mid4[x]
        for d in (1, 3, 2):
            x_last(d).wait_recv()
            total += got_x[last, d, 0]
        out_ref[:, pl.ds(last * TILE, TILE)] = total

    def one_tile(t):
        def past(bound):
            return (t >= bound).astype(jnp.int32)

        left = past(4) + past(7) + past(9)
        low = t - 4 * past(4) - 3 * past(7) - 2 * past(9) + left

        @pl.when(t == 0)
        def _():
            rest.wait()

        @pl.when((t > 0) & (t < GROUPS))
        def _():
            load(t).wait()

        rows = pl.ds(pl.multiple_of(low * TILE, TILE), TILE)
        columns = pl.ds(pl.multiple_of(left * TILE, TILE), TILE)
        tile = outer(a_v[rows, :], a_v[columns, :])
        acc[left, pl.ds(low * 2, 2)] = tile.reshape(2, 2, 64, TILE)
        acc[low, pl.ds(left * 2, 2)] = tile.T.reshape(2, 2, 64, TILE)

        @pl.when(low == GROUPS - 1)
        def _():
            pair_of(left).start()

        @pl.when((t != 0) & (t != 3) & (t != 7))
        def _():
            forward(t - 1 - past(4) - past(8))

        @pl.when((t == 4) | (t == 7) | (t == 9))
        def _():
            exchange_x(past(5) + past(8))

    loop(0, 10, one_tile)

    def strip_chunk(i):
        near(i).wait_recv()
        tile = outer(a_v[:, cols(i)], strip[i])
        acc_s[...] += tile.reshape(CHIPS, 2, 64, SLOT)

    @pl.when(tm < TM - 1)
    def _():
        send_packed.wait_recv()
        packed = packed_dst[...].astype(jnp.float32)
        for p in range(PIECES):
            part_p = packed if p == 0 else pltpu.roll(packed, 16 - REST * p, 0)
            part_p = jnp.where(rows16 < REST, part_p, 0.0)
            part_p = part_p.astype(jnp.bfloat16)
            for k in range(piece // width):
                strip[p * (piece // width) + k, BULK : BULK + 16] = part_p[
                    :, k * width : (k + 1) * width
                ]

    def one_chunk(pos):
        @pl.when(tm < TM - 1)
        def _():
            late = pos - HALF
            chunk = jnp.where(late < 0, pos, HALF + late // 2 + LONG * (late % 2))
            strip_chunk(chunk)

        @pl.when((pos == 0) | (pos == 2) | (pos == 6))
        def _():
            forward(7 + (pos > 1).astype(jnp.int32) + (pos > 5).astype(jnp.int32))

        @pl.when(pos == 1)
        def _():
            last_z()

        @pl.when(pos == 12)
        def _():
            last_x()

        @pl.when((pos == 3) | (pos == 8) | (pos == 14))
        def _():
            exchange_z((pos > 4).astype(jnp.int32) + (pos > 10).astype(jnp.int32))

    loop(0, CHUNKS, one_chunk)

    def s_pair():
        src = acc_s.at[:, 1 - core]
        return remote(src, pair_s, s_sem.at[0, 0], s_sem.at[1, 0], partner)

    def s_of(d):
        other = (zh + d // 4) % 2 * 4 + (x + d) % 4
        src, dst = part_s.at[other], got_s.at[d]
        return remote(src, dst, s_sem.at[0, d], s_sem.at[1, d], peer(other))

    s_pair().start()
    s_pair().wait_recv()
    for q in range(CHIPS):
        part_s[q] = acc_s[q, core] + pair_s[q]
    for d in (6, 5, 7, 2, 4, 1, 3):
        s_of(d).start()
    loop(0, last, finish)
    last_finish()
    total = part_s[chip]
    for d in (1, 3, 4, 2, 5, 7, 6):
        s_of(d).wait_recv()
        total += got_s[d]
    out_ref[:, pl.ds(GROUPS * TILE, SLOT)] = total

    @pl.when(tm > 0)
    def _():
        send_packed.wait_send()

    def ended(i):
        @pl.when((tm > 0) & ((tm != 4) | (i < HALF)))
        def _():
            near(i).wait_send()

    loop(0, NEAR, ended)

    def ended_long(k):
        @pl.when(sends1)
        def _():
            hop1(k).wait_send()

        @pl.when(sends2)
        def _():
            hop2(k).wait_send()

        @pl.when(sends3)
        def _():
            hop3(k).wait_send()

    loop(0, LONG, ended_long)

    def ended_via(k):
        @pl.when(tm == 4)
        def _():
            via1(k).wait_send()

        @pl.when(tm == 0)
        def _():
            via2(k).wait_send()

    loop(0, HALF, ended_via)

    def ended_group(g):
        z_of(g).wait_send()
        for d in range(1, 4):
            x_of(g, d).wait_send()

    loop(0, last, ended_group)
    z_first().wait_send()
    for d in range(1, 4):
        x_last(d).wait_send()
    loop(0, GROUPS, lambda g: pair_of(g).wait_send())
    s_pair().wait_send()
    for d in range(1, CHIPS):
        s_of(d).wait_send()


def on_device(snapshots):
    snap, depth = snapshots.shape
    mine = snap // lax.axis_size("row")
    total_rows = depth * lax.axis_size("row")
    columns = snap + LAG - 1
    width = depth // CHUNKS
    f32, bf16 = jnp.float32, jnp.bfloat16
    dma = pltpu.SemaphoreType.DMA
    summed = pl.pallas_call(
        kernel,
        out_shape=jax.ShapeDtypeStruct((mine, snap + SLOT), f32),
        in_specs=[pl.BlockSpec(memory_space=pl.ANY)],
        out_specs=pl.BlockSpec(memory_space=pltpu.VMEM),
        scratch_shapes=[
            pltpu.VMEM((snap, depth), bf16),
            pltpu.VMEM((16, depth // PIECES), bf16),
            pltpu.VMEM((16, depth // PIECES), bf16),
            pltpu.VMEM((CHUNKS, SLOT, width), bf16),
            pltpu.VMEM((LONG, BULK, width), bf16),
            pltpu.VMEM((LONG, BULK, width), bf16),
            pltpu.VMEM((HALF, BULK, width), bf16),
            pltpu.VMEM((GROUPS, CHIPS, 2, mine, TILE), f32),
            pltpu.VMEM((CHIPS, 2, mine, SLOT), f32),
            pltpu.VMEM((GROUPS, CHIPS, mine, TILE), f32),
            pltpu.VMEM((CHIPS, mine, SLOT), f32),
            pltpu.VMEM((GROUPS, 2, 4, mine, TILE), f32),
            pltpu.VMEM((CHIPS, mine, SLOT), f32),
            pltpu.VMEM((GROUPS, 4, 2, mine, TILE), f32),
            pltpu.VMEM((GROUPS, 2, mine, TILE), f32),
            pltpu.VMEM((GROUPS, mine, TILE), f32),
            pltpu.VMEM((4, mine, TILE), f32),
            pltpu.VMEM((4, mine, TILE), f32),
            pltpu.VMEM((CHIPS, mine, SLOT), f32),
            dma((GROUPS,)),
            dma((2,)),
            dma((CHUNKS,)),
            dma((CHUNKS,)),
            dma((2,)),
            dma((2, LONG)),
            dma((2, LONG)),
            dma((LONG,)),
            dma((2, HALF)),
            dma((HALF,)),
            dma((2, GROUPS)),
            dma((2, GROUPS, 4)),
            dma((2, GROUPS)),
            dma((2, CHIPS)),
        ],
        compiler_params=pltpu.CompilerParams(
            collective_id=0, has_side_effects=True, vmem_limit_bytes=56 * 2**20
        ),
        name="lagged_gram",
    )(snapshots)
    return summed[:, :columns] * (1.0 / total_rows)


def solution(mesh):
    return jax.shard_map(
        on_device,
        mesh=mesh,
        in_specs=(P("tm", "row"),),
        out_specs=P(("tm", "row"), None),
        check_vma=False,
    )
```

```python
import jax
import jax.numpy as jnp
from jax import lax
from jax.experimental import pallas as pl
from jax.experimental.pallas import tpu as pltpu
from jax.sharding import PartitionSpec as P

MESH = pl.DeviceIdType.MESH
LAG = 100
CHIPS = 8
TM = 8
TILE = 256
GROUPS = 4
BULK = 96
REST = LAG - 1 - BULK
PIECES = 5
SLOT = 128
CHUNKS = 20
LONG = 5
HALF = CHUNKS // 2
NEAR = CHUNKS - LONG
NT = (((1,), (1,)), ((), ()))


def outer(left, right):
    return lax.dot_general(left, right, NT, preferred_element_type=jnp.float32)


def loop(start, stop, body):
    def step(i, carry):
        body(i)
        return carry

    lax.fori_loop(start, stop, step, 0)


def kernel(
    a_ref,
    out_ref,
    a_v,
    packed_src,
    packed_dst,
    strip,
    first,
    second,
    via,
    acc,
    acc_s,
    pair,
    pair_s,
    part,
    part_s,
    got_x,
    mid,
    got_z,
    mid4,
    got_z4,
    got_s,
    load_sem,
    tail_sem,
    strip_send,
    strip_recv,
    packed_sem,
    first_sem,
    second_sem,
    third_send,
    via_sem,
    away_send,
    pair_sem,
    x_sem,
    z_sem,
    s_sem,
):
    depth = a_v.shape[1]
    row, tm = lax.axis_index("row"), lax.axis_index("tm")
    chip, core = row // 2, row % 2
    zh, x = chip // 4, chip % 4
    zl, y = tm // 4, tm % 4
    partner = (chip * 2 + 1 - core, tm)
    before = (row, (tm + TM - 1) % TM)
    up = (row, zl * 4 + (y + 1) % 4)
    down = (row, zl * 4 + (y + 3) % 4)

    def peer(other):
        return (other * 2 + core, tm)

    def remote(src, dst, send, recv, device):
        return pltpu.make_async_remote_copy(
            src_ref=src,
            dst_ref=dst,
            send_sem=send,
            recv_sem=recv,
            device_id=device,
            device_id_type=MESH,
        )

    def load_rows(start, size, sem):
        rows = pl.ds(start, size)
        return pltpu.make_async_copy(a_ref.at[rows], a_v.at[rows], sem)

    head = load_rows(0, SLOT, tail_sem.at[0])
    rest = load_rows(SLOT, TILE - SLOT, tail_sem.at[1])
    head.start()

    def load(block):
        rows = pl.ds(pl.multiple_of(block * TILE, TILE), TILE)
        return pltpu.make_async_copy(a_ref.at[rows], a_v.at[rows], load_sem.at[block])

    barrier = pltpu.get_barrier_semaphore()

    def greet(device):
        pl.semaphore_signal(barrier, inc=1, device_id=device, device_id_type=MESH)

    greet(up)
    greet(down)
    greet(partner)
    for d in range(1, CHIPS):
        greet(peer((chip + d) % CHIPS))

    @pl.when(tm == 0)
    def _():
        greet((row, 4))

    @pl.when(tm == 3)
    def _():
        greet((row, 4))

    @pl.when(tm == 4)
    def _():
        greet((row, 0))
        greet((row, 3))

    head.wait()
    rest.start()
    loop(1, GROUPS, lambda block: load(block).start())
    more = (tm == 0).astype(jnp.int32) + (tm == 3).astype(jnp.int32)
    more = more + 2 * (tm == 4).astype(jnp.int32)
    pl.semaphore_wait(barrier, CHIPS + 2 + more)

    width = depth // CHUNKS

    def cols(i):
        return pl.ds(pl.multiple_of(i * width, width), width)

    def source(i):
        return a_v.at[pl.ds(0, BULK), cols(i)]

    def landing(i):
        half = pl.ds(pl.multiple_of(i % 2 * width, width), width)
        return strip.at[i // 2, pl.ds(0, BULK), half]

    def near(i):
        return remote(source(i), landing(i), strip_send.at[i], strip_recv.at[i], before)

    def hop1(k):
        dst = first.at[k]
        return remote(source(NEAR + k), dst, first_sem.at[0, k], first_sem.at[1, k], up)

    def hop2(k):
        src, dst = first.at[k], second.at[k]
        return remote(src, dst, second_sem.at[0, k], second_sem.at[1, k], up)

    def hop3(k):
        src, dst = second.at[k], landing(NEAR + k)
        return remote(src, dst, third_send.at[k], strip_recv.at[NEAR + k], up)

    def via1(k):
        dst = via.at[k]
        return remote(source(HALF + k), dst, via_sem.at[0, k], via_sem.at[1, k], (row, 0))

    def via2(k):
        src, dst = via.at[k], landing(HALF + k)
        return remote(src, dst, away_send.at[k], strip_recv.at[HALF + k], (row, 3))

    send_packed = remote(
        packed_src, packed_dst, packed_sem.at[0], packed_sem.at[1], before
    )
    sends1, sends2, sends3 = y != 0, y != 1, y != 2

    def begin(i):
        @pl.when(tm > 0)
        def _():
            near(i).start()

        @pl.when(sends1 & (i < LONG))
        def _():
            hop1(i).start()

        @pl.when(tm == 4)
        def _():
            via1(i).start()

    def begin_rest(i):
        @pl.when((tm > 0) & (tm != 4))
        def _():
            near(i).start()

    loop(0, 2, begin)

    piece = depth // PIECES
    rows16 = lax.broadcasted_iota(jnp.int32, (16, piece), 0)
    packed = jnp.zeros((16, piece), jnp.float32)
    for p in range(PIECES):
        part_p = a_v[BULK : BULK + 16, p * piece : (p + 1) * piece].astype(jnp.float32)
        part_p = jnp.where(rows16 < REST, part_p, 0.0)
        packed += part_p if p == 0 else pltpu.roll(part_p, REST * p, 0)
    packed_src[...] = packed.astype(jnp.bfloat16)

    @pl.when(tm > 0)
    def _():
        send_packed.start()

    loop(2, HALF, begin)
    loop(HALF, NEAR, begin_rest)

    acc_s[...] = jnp.zeros_like(acc_s)
    strip[:, BULK + 16 :, :] = jnp.zeros(
        (CHUNKS // 2, SLOT - BULK - 16, 2 * width), jnp.bfloat16
    )

    def forward(p):
        @pl.when(sends2 & (p < LONG))
        def _():
            hop1(p).wait_recv()
            hop2(p).start()

        @pl.when(sends3 & (p >= LONG))
        def _():
            hop2(p - LONG).wait_recv()
            hop3(p - LONG).start()

        @pl.when(tm == 0)
        def _():
            via1(p).wait_recv()
            via2(p).start()

    def pair_of(g):
        src = acc.at[g, :, 1 - core]
        return remote(src, pair.at[g], pair_sem.at[0, g], pair_sem.at[1, g], partner)

    def x_of(g, d):
        other = (x + d) % 4
        src, dst = part.at[g, :, other], got_x.at[g, d]
        return remote(
            src, dst, x_sem.at[0, g, d], x_sem.at[1, g, d], peer(zh * 4 + other)
        )

    def z_of(g):
        src, dst = mid.at[g, 1 - zh], got_z.at[g]
        return remote(
            src, dst, z_sem.at[0, g], z_sem.at[1, g], peer((1 - zh) * 4 + x)
        )

    last = GROUPS - 1

    def sum_pair(g):
        pair_of(g).wait_recv()
        for q in range(CHIPS):
            part[g, q // 4, q % 4] = acc[g, q, core] + pair[g, q]

    def exchange_x(g):
        sum_pair(g)
        for d in (2, 1, 3):
            x_of(g, d).start()

    def exchange_z(g):
        for d in (1, 3, 2):
            x_of(g, d).wait_recv()
        for half in range(2):
            total = part[g, half, x]
            for d in range(1, 4):
                total += got_x[g, d, half]
            mid[g, half] = total
        z_of(g).start()

    def finish(g):
        z_of(g).wait_recv()
        columns = pl.ds(pl.multiple_of(g * TILE, TILE), TILE)
        out_ref[:, columns] = mid[g, zh] + got_z[g]

    def z_first():
        src = part.at[last, 1 - zh]
        return remote(
            src, got_z4, z_sem.at[0, last], z_sem.at[1, last], peer((1 - zh) * 4 + x)
        )

    def x_last(d):
        other = (x + d) % 4
        return remote(
            mid4.at[other],
            got_x.at[last, d, 0],
            x_sem.at[0, last, d],
            x_sem.at[1, last, d],
            peer(zh * 4 + other),
        )

    def last_z():
        sum_pair(last)
        z_first().start()

    def last_x():
        z_first().wait_recv()
        for q in range(4):
            mid4[q] = part[last, zh, q] + got_z4[q]
        for d in (2, 1, 3):
            x_last(d).start()

    def last_finish():
        total = mid4[x]
        for d in (1, 3, 2):
            x_last(d).wait_recv()
            total += got_x[last, d, 0]
        out_ref[:, pl.ds(last * TILE, TILE)] = total

    def one_tile(t):
        def past(bound):
            return (t >= bound).astype(jnp.int32)

        left = past(4) + past(7) + past(9)
        low = t - 4 * past(4) - 3 * past(7) - 2 * past(9) + left

        @pl.when(t == 0)
        def _():
            rest.wait()

        @pl.when((t > 0) & (t < GROUPS))
        def _():
            load(t).wait()

        rows = pl.ds(pl.multiple_of(low * TILE, TILE), TILE)
        columns = pl.ds(pl.multiple_of(left * TILE, TILE), TILE)
        tile = outer(a_v[rows, :], a_v[columns, :])
        acc[left, pl.ds(low * 2, 2)] = tile.reshape(2, 2, 64, TILE)
        acc[low, pl.ds(left * 2, 2)] = tile.T.reshape(2, 2, 64, TILE)

        @pl.when(low == GROUPS - 1)
        def _():
            pair_of(left).start()

        @pl.when((t != 0) & (t != 3) & (t != 7))
        def _():
            forward(t - 1 - past(4) - past(8))

        @pl.when((t == 4) | (t == 7) | (t == 9))
        def _():
            exchange_x(past(5) + past(8))

    loop(0, 10, one_tile)

    def strip_chunk(i):
        near(i).wait_recv()
        tile = outer(
            a_v[:, cols(i)],
            strip[i // 2, :, pl.ds(pl.multiple_of(i % 2 * width, width), width)],
        )
        acc_s[...] += tile.reshape(CHIPS, 2, 64, SLOT)

    def strip_double(i):
        near(2 * i).wait_recv()
        near(2 * i + 1).wait_recv()
        wide = pl.ds(pl.multiple_of(i * 2 * width, 2 * width), 2 * width)
        tile = outer(a_v[:, wide], strip[i])
        acc_s[...] += tile.reshape(CHIPS, 2, 64, SLOT)

    @pl.when(tm < TM - 1)
    def _():
        send_packed.wait_recv()
        packed = packed_dst[...].astype(jnp.float32)
        for p in range(PIECES):
            part_p = packed if p == 0 else pltpu.roll(packed, 16 - REST * p, 0)
            part_p = jnp.where(rows16 < REST, part_p, 0.0)
            part_p = part_p.astype(jnp.bfloat16)
            for k in range(2):
                strip[2 * p + k, BULK : BULK + 16] = part_p[
                    :, k * 2 * width : (k + 1) * 2 * width
                ]

    def one_chunk(pos):
        @pl.when((tm < TM - 1) & (pos < HALF) & (pos % 2 == 1))
        def _():
            strip_double(pos // 2)

        @pl.when((tm < TM - 1) & (pos >= HALF))
        def _():
            late = pos - HALF
            strip_chunk(HALF + late // 2 + LONG * (1 - late % 2))

        @pl.when((pos == 0) | (pos == 2) | (pos == 6))
        def _():
            forward(7 + (pos > 1).astype(jnp.int32) + (pos > 5).astype(jnp.int32))

        @pl.when(pos == 1)
        def _():
            last_z()

        @pl.when(pos == 12)
        def _():
            last_x()

        @pl.when((pos == 3) | (pos == 8) | (pos == 14))
        def _():
            exchange_z((pos > 4).astype(jnp.int32) + (pos > 10).astype(jnp.int32))

    loop(0, CHUNKS, one_chunk)

    def s_pair():
        src = acc_s.at[:, 1 - core]
        return remote(src, pair_s, s_sem.at[0, 0], s_sem.at[1, 0], partner)

    def s_of(d):
        other = (zh + d // 4) % 2 * 4 + (x + d) % 4
        src, dst = part_s.at[other], got_s.at[d]
        return remote(src, dst, s_sem.at[0, d], s_sem.at[1, d], peer(other))

    s_pair().start()
    s_pair().wait_recv()
    for q in range(CHIPS):
        part_s[q] = acc_s[q, core] + pair_s[q]
    for d in (6, 5, 7, 2, 4, 1, 3):
        s_of(d).start()
    loop(0, last, finish)
    last_finish()
    total = part_s[chip]
    for d in (1, 3, 4, 2, 5, 7, 6):
        s_of(d).wait_recv()
        total += got_s[d]
    out_ref[:, pl.ds(GROUPS * TILE, SLOT)] = total

    @pl.when(tm > 0)
    def _():
        send_packed.wait_send()

    def ended(i):
        @pl.when((tm > 0) & ((tm != 4) | (i < HALF)))
        def _():
            near(i).wait_send()

    loop(0, NEAR, ended)

    def ended_long(k):
        @pl.when(sends1)
        def _():
            hop1(k).wait_send()

        @pl.when(sends2)
        def _():
            hop2(k).wait_send()

        @pl.when(sends3)
        def _():
            hop3(k).wait_send()

    loop(0, LONG, ended_long)

    def ended_via(k):
        @pl.when(tm == 4)
        def _():
            via1(k).wait_send()

        @pl.when(tm == 0)
        def _():
            via2(k).wait_send()

    loop(0, HALF, ended_via)

    def ended_group(g):
        z_of(g).wait_send()
        for d in range(1, 4):
            x_of(g, d).wait_send()

    loop(0, last, ended_group)
    z_first().wait_send()
    for d in range(1, 4):
        x_last(d).wait_send()
    loop(0, GROUPS, lambda g: pair_of(g).wait_send())
    s_pair().wait_send()
    for d in range(1, CHIPS):
        s_of(d).wait_send()


def on_device(snapshots):
    snap, depth = snapshots.shape
    mine = snap // lax.axis_size("row")
    total_rows = depth * lax.axis_size("row")
    columns = snap + LAG - 1
    width = depth // CHUNKS
    f32, bf16 = jnp.float32, jnp.bfloat16
    dma = pltpu.SemaphoreType.DMA
    summed = pl.pallas_call(
        kernel,
        out_shape=jax.ShapeDtypeStruct((mine, snap + SLOT), f32),
        in_specs=[pl.BlockSpec(memory_space=pl.ANY)],
        out_specs=pl.BlockSpec(memory_space=pltpu.VMEM),
        scratch_shapes=[
            pltpu.VMEM((snap, depth), bf16),
            pltpu.VMEM((16, depth // PIECES), bf16),
            pltpu.VMEM((16, depth // PIECES), bf16),
            pltpu.VMEM((CHUNKS // 2, SLOT, 2 * width), bf16),
            pltpu.VMEM((LONG, BULK, width), bf16),
            pltpu.VMEM((LONG, BULK, width), bf16),
            pltpu.VMEM((HALF, BULK, width), bf16),
            pltpu.VMEM((GROUPS, CHIPS, 2, mine, TILE), f32),
            pltpu.VMEM((CHIPS, 2, mine, SLOT), f32),
            pltpu.VMEM((GROUPS, CHIPS, mine, TILE), f32),
            pltpu.VMEM((CHIPS, mine, SLOT), f32),
            pltpu.VMEM((GROUPS, 2, 4, mine, TILE), f32),
            pltpu.VMEM((CHIPS, mine, SLOT), f32),
            pltpu.VMEM((GROUPS, 4, 2, mine, TILE), f32),
            pltpu.VMEM((GROUPS, 2, mine, TILE), f32),
            pltpu.VMEM((GROUPS, mine, TILE), f32),
            pltpu.VMEM((4, mine, TILE), f32),
            pltpu.VMEM((4, mine, TILE), f32),
            pltpu.VMEM((CHIPS, mine, SLOT), f32),
            dma((GROUPS,)),
            dma((2,)),
            dma((CHUNKS,)),
            dma((CHUNKS,)),
            dma((2,)),
            dma((2, LONG)),
            dma((2, LONG)),
            dma((LONG,)),
            dma((2, HALF)),
            dma((HALF,)),
            dma((2, GROUPS)),
            dma((2, GROUPS, 4)),
            dma((2, GROUPS)),
            dma((2, CHIPS)),
        ],
        compiler_params=pltpu.CompilerParams(
            collective_id=0, has_side_effects=True, vmem_limit_bytes=56 * 2**20
        ),
        name="lagged_gram",
    )(snapshots)
    return summed[:, :columns] * (1.0 / total_rows)


def solution(mesh):
    return jax.shard_map(
        on_device,
        mesh=mesh,
        in_specs=(P("tm", "row"),),
        out_specs=P(("tm", "row"), None),
        check_vma=False,
    )
```

```python
import jax
import jax.numpy as jnp
from jax import lax
from jax.experimental import pallas as pl
from jax.experimental.pallas import tpu as pltpu
from jax.sharding import PartitionSpec as P

MESH = pl.DeviceIdType.MESH
LAG = 100
CHIPS = 8
TM = 8
TILE = 256
GROUPS = 4
BULK = 96
REST = LAG - 1 - BULK
PIECES = 5
SLOT = 128
CHUNKS = 20
LONG = 5
HALF = CHUNKS // 2
NEAR = CHUNKS - LONG
NT = (((1,), (1,)), ((), ()))


def outer(left, right):
    return lax.dot_general(left, right, NT, preferred_element_type=jnp.float32)


def loop(start, stop, body):
    def step(i, carry):
        body(i)
        return carry

    lax.fori_loop(start, stop, step, 0)


def kernel(
    a_ref,
    out_ref,
    a_v,
    packed_src,
    packed_dst,
    strip,
    first,
    second,
    via,
    acc,
    acc_s,
    pair,
    pair_s,
    part,
    part_s,
    got_x,
    mid,
    got_z,
    mid4,
    got_z4,
    got_s,
    load_sem,
    tail_sem,
    strip_send,
    strip_recv,
    packed_sem,
    first_sem,
    second_sem,
    third_send,
    via_sem,
    away_send,
    pair_sem,
    x_sem,
    z_sem,
    s_sem,
):
    depth = a_v.shape[1]
    row, tm = lax.axis_index("row"), lax.axis_index("tm")
    chip, core = row // 2, row % 2
    zh, x = chip // 4, chip % 4
    zl, y = tm // 4, tm % 4
    partner = (chip * 2 + 1 - core, tm)
    before = (row, (tm + TM - 1) % TM)
    up = (row, zl * 4 + (y + 1) % 4)
    down = (row, zl * 4 + (y + 3) % 4)

    def peer(other):
        return (other * 2 + core, tm)

    def remote(src, dst, send, recv, device):
        return pltpu.make_async_remote_copy(
            src_ref=src,
            dst_ref=dst,
            send_sem=send,
            recv_sem=recv,
            device_id=device,
            device_id_type=MESH,
        )

    def load_rows(start, size, sem):
        rows = pl.ds(start, size)
        return pltpu.make_async_copy(a_ref.at[rows], a_v.at[rows], sem)

    head = load_rows(0, SLOT, tail_sem.at[0])
    rest = load_rows(SLOT, TILE - SLOT, tail_sem.at[1])
    head.start()

    def load(block):
        rows = pl.ds(pl.multiple_of(block * TILE, TILE), TILE)
        return pltpu.make_async_copy(a_ref.at[rows], a_v.at[rows], load_sem.at[block])

    barrier = pltpu.get_barrier_semaphore()

    def greet(device):
        pl.semaphore_signal(barrier, inc=1, device_id=device, device_id_type=MESH)

    greet(up)
    greet(down)
    greet(partner)
    for d in range(1, CHIPS):
        greet(peer((chip + d) % CHIPS))

    @pl.when(tm == 0)
    def _():
        greet((row, 4))

    @pl.when(tm == 3)
    def _():
        greet((row, 4))

    @pl.when(tm == 4)
    def _():
        greet((row, 0))
        greet((row, 3))

    head.wait()
    rest.start()
    loop(1, GROUPS, lambda block: load(block).start())
    more = (tm == 0).astype(jnp.int32) + (tm == 3).astype(jnp.int32)
    more = more + 2 * (tm == 4).astype(jnp.int32)
    pl.semaphore_wait(barrier, CHIPS + 2 + more)

    width = depth // CHUNKS

    def cols(i):
        return pl.ds(pl.multiple_of(i * width, width), width)

    def source(i):
        return a_v.at[pl.ds(0, BULK), cols(i)]

    def landing(i):
        half = pl.ds(pl.multiple_of(i % 2 * width, width), width)
        return strip.at[i // 2, pl.ds(0, BULK), half]

    def near(i):
        return remote(source(i), landing(i), strip_send.at[i], strip_recv.at[i], before)

    def hop1(k):
        dst = first.at[k]
        return remote(source(NEAR + k), dst, first_sem.at[0, k], first_sem.at[1, k], up)

    def hop2(k):
        src, dst = first.at[k], second.at[k]
        return remote(src, dst, second_sem.at[0, k], second_sem.at[1, k], up)

    def hop3(k):
        src, dst = second.at[k], landing(NEAR + k)
        return remote(src, dst, third_send.at[k], strip_recv.at[NEAR + k], up)

    def via1(k):
        dst = via.at[k]
        return remote(source(HALF + k), dst, via_sem.at[0, k], via_sem.at[1, k], (row, 0))

    def via2(k):
        src, dst = via.at[k], landing(HALF + k)
        return remote(src, dst, away_send.at[k], strip_recv.at[HALF + k], (row, 3))

    send_packed = remote(
        packed_src, packed_dst, packed_sem.at[0], packed_sem.at[1], before
    )
    sends1, sends2, sends3 = y != 0, y != 1, y != 2

    def begin(i):
        @pl.when(sends1 & (i < LONG))
        def _():
            hop1(i).start()

        @pl.when(tm > 0)
        def _():
            near(i).start()

        @pl.when(tm == 4)
        def _():
            via1(i).start()

    def begin_rest(i):
        @pl.when((tm > 0) & (tm != 4))
        def _():
            near(i).start()

    loop(0, 2, begin)

    piece = depth // PIECES
    rows16 = lax.broadcasted_iota(jnp.int32, (16, piece), 0)
    packed = jnp.zeros((16, piece), jnp.float32)
    for p in range(PIECES):
        part_p = a_v[BULK : BULK + 16, p * piece : (p + 1) * piece].astype(jnp.float32)
        part_p = jnp.where(rows16 < REST, part_p, 0.0)
        packed += part_p if p == 0 else pltpu.roll(part_p, REST * p, 0)
    packed_src[...] = packed.astype(jnp.bfloat16)

    @pl.when(tm > 0)
    def _():
        send_packed.start()

    loop(2, HALF, begin)
    loop(HALF, NEAR, begin_rest)

    acc_s[...] = jnp.zeros_like(acc_s)
    strip[:, BULK + 16 :, :] = jnp.zeros(
        (CHUNKS // 2, SLOT - BULK - 16, 2 * width), jnp.bfloat16
    )

    def forward(p):
        @pl.when(sends2 & (p < LONG))
        def _():
            hop1(p).wait_recv()
            hop2(p).start()

        @pl.when(sends3 & (p >= LONG))
        def _():
            hop2(p - LONG).wait_recv()
            hop3(p - LONG).start()

        @pl.when(tm == 0)
        def _():
            via1(p).wait_recv()
            via2(p).start()

    def pair_of(g):
        src = acc.at[g, :, 1 - core]
        return remote(src, pair.at[g], pair_sem.at[0, g], pair_sem.at[1, g], partner)

    def x_of(g, d):
        other = (x + d) % 4
        src, dst = part.at[g, :, other], got_x.at[g, d]
        return remote(
            src, dst, x_sem.at[0, g, d], x_sem.at[1, g, d], peer(zh * 4 + other)
        )

    def z_of(g):
        src, dst = mid.at[g, 1 - zh], got_z.at[g]
        return remote(
            src, dst, z_sem.at[0, g], z_sem.at[1, g], peer((1 - zh) * 4 + x)
        )

    last = GROUPS - 1

    def sum_pair(g):
        pair_of(g).wait_recv()
        for q in range(CHIPS):
            part[g, q // 4, q % 4] = acc[g, q, core] + pair[g, q]

    def exchange_x(g):
        sum_pair(g)
        for d in (2, 1, 3):
            x_of(g, d).start()

    def exchange_z(g):
        for d in (1, 3, 2):
            x_of(g, d).wait_recv()
        for half in range(2):
            total = part[g, half, x]
            for d in range(1, 4):
                total += got_x[g, d, half]
            mid[g, half] = total
        z_of(g).start()

    def finish(g):
        z_of(g).wait_recv()
        columns = pl.ds(pl.multiple_of(g * TILE, TILE), TILE)
        out_ref[:, columns] = mid[g, zh] + got_z[g]

    def z_first():
        src = part.at[last, 1 - zh]
        return remote(
            src, got_z4, z_sem.at[0, last], z_sem.at[1, last], peer((1 - zh) * 4 + x)
        )

    def x_last(d):
        other = (x + d) % 4
        return remote(
            mid4.at[other],
            got_x.at[last, d, 0],
            x_sem.at[0, last, d],
            x_sem.at[1, last, d],
            peer(zh * 4 + other),
        )

    def last_z():
        sum_pair(last)
        z_first().start()

    def last_x():
        z_first().wait_recv()
        for q in range(4):
            mid4[q] = part[last, zh, q] + got_z4[q]
        for d in (2, 1, 3):
            x_last(d).start()

    def last_finish():
        total = mid4[x]
        for d in (1, 3, 2):
            x_last(d).wait_recv()
            total += got_x[last, d, 0]
        out_ref[:, pl.ds(last * TILE, TILE)] = total

    def one_tile(t):
        def past(bound):
            return (t >= bound).astype(jnp.int32)

        left = past(4) + past(7) + past(9)
        low = t - 4 * past(4) - 3 * past(7) - 2 * past(9) + left

        @pl.when(t == 0)
        def _():
            rest.wait()

        @pl.when((t > 0) & (t < GROUPS))
        def _():
            load(t).wait()

        rows = pl.ds(pl.multiple_of(low * TILE, TILE), TILE)
        columns = pl.ds(pl.multiple_of(left * TILE, TILE), TILE)
        tile = outer(a_v[rows, :], a_v[columns, :])
        acc[left, pl.ds(low * 2, 2)] = tile.reshape(2, 2, 64, TILE)
        acc[low, pl.ds(left * 2, 2)] = tile.T.reshape(2, 2, 64, TILE)

        @pl.when(low == GROUPS - 1)
        def _():
            pair_of(left).start()

        @pl.when((t != 0) & (t != 3) & (t != 7))
        def _():
            forward(t - 1 - past(4) - past(8))

        @pl.when((t == 4) | (t == 7) | (t == 9))
        def _():
            exchange_x(past(5) + past(8))

    loop(0, 10, one_tile)

    def strip_chunk(i):
        near(i).wait_recv()
        tile = outer(
            a_v[:, cols(i)],
            strip[i // 2, :, pl.ds(pl.multiple_of(i % 2 * width, width), width)],
        )
        acc_s[...] += tile.reshape(CHIPS, 2, 64, SLOT)

    def strip_double(i):
        near(2 * i).wait_recv()
        near(2 * i + 1).wait_recv()
        wide = pl.ds(pl.multiple_of(i * 2 * width, 2 * width), 2 * width)
        tile = outer(a_v[:, wide], strip[i])
        acc_s[...] += tile.reshape(CHIPS, 2, 64, SLOT)

    @pl.when(tm < TM - 1)
    def _():
        send_packed.wait_recv()
        packed = packed_dst[...].astype(jnp.float32)
        for p in range(PIECES):
            part_p = packed if p == 0 else pltpu.roll(packed, 16 - REST * p, 0)
            part_p = jnp.where(rows16 < REST, part_p, 0.0)
            part_p = part_p.astype(jnp.bfloat16)
            for k in range(2):
                strip[2 * p + k, BULK : BULK + 16] = part_p[
                    :, k * 2 * width : (k + 1) * 2 * width
                ]

    def one_chunk(pos):
        @pl.when((tm < TM - 1) & (pos < HALF) & (pos % 2 == 1))
        def _():
            strip_double(pos // 2)

        @pl.when((tm < TM - 1) & (pos >= HALF))
        def _():
            late = pos - HALF
            strip_chunk(HALF + late // 2 + LONG * (1 - late % 2))

        @pl.when((pos == 0) | (pos == 2) | (pos == 6))
        def _():
            forward(7 + (pos > 1).astype(jnp.int32) + (pos > 5).astype(jnp.int32))

        @pl.when(pos == 1)
        def _():
            last_z()

        @pl.when(pos == 12)
        def _():
            last_x()

        @pl.when((pos == 3) | (pos == 8) | (pos == 14))
        def _():
            exchange_z((pos > 4).astype(jnp.int32) + (pos > 10).astype(jnp.int32))

    loop(0, CHUNKS, one_chunk)

    def s_pair():
        src = acc_s.at[:, 1 - core]
        return remote(src, pair_s, s_sem.at[0, 0], s_sem.at[1, 0], partner)

    def s_of(d):
        other = (zh + d // 4) % 2 * 4 + (x + d) % 4
        src, dst = part_s.at[other], got_s.at[d]
        return remote(src, dst, s_sem.at[0, d], s_sem.at[1, d], peer(other))

    s_pair().start()
    s_pair().wait_recv()
    for q in range(CHIPS):
        part_s[q] = acc_s[q, core] + pair_s[q]
    for d in (6, 5, 7, 2, 4, 1, 3):
        s_of(d).start()
    loop(0, last, finish)
    last_finish()
    total = part_s[chip]
    for d in (1, 3, 4, 2, 5, 7, 6):
        s_of(d).wait_recv()
        total += got_s[d]
    out_ref[:, pl.ds(GROUPS * TILE, SLOT)] = total

    @pl.when(tm > 0)
    def _():
        send_packed.wait_send()

    def ended(i):
        @pl.when((tm > 0) & ((tm != 4) | (i < HALF)))
        def _():
            near(i).wait_send()

    loop(0, NEAR, ended)

    def ended_long(k):
        @pl.when(sends1)
        def _():
            hop1(k).wait_send()

        @pl.when(sends2)
        def _():
            hop2(k).wait_send()

        @pl.when(sends3)
        def _():
            hop3(k).wait_send()

    loop(0, LONG, ended_long)

    def ended_via(k):
        @pl.when(tm == 4)
        def _():
            via1(k).wait_send()

        @pl.when(tm == 0)
        def _():
            via2(k).wait_send()

    loop(0, HALF, ended_via)

    def ended_group(g):
        z_of(g).wait_send()
        for d in range(1, 4):
            x_of(g, d).wait_send()

    loop(0, last, ended_group)
    z_first().wait_send()
    for d in range(1, 4):
        x_last(d).wait_send()
    loop(0, GROUPS, lambda g: pair_of(g).wait_send())
    s_pair().wait_send()
    for d in range(1, CHIPS):
        s_of(d).wait_send()


def on_device(snapshots):
    snap, depth = snapshots.shape
    mine = snap // lax.axis_size("row")
    total_rows = depth * lax.axis_size("row")
    columns = snap + LAG - 1
    width = depth // CHUNKS
    f32, bf16 = jnp.float32, jnp.bfloat16
    dma = pltpu.SemaphoreType.DMA
    summed = pl.pallas_call(
        kernel,
        out_shape=jax.ShapeDtypeStruct((mine, snap + SLOT), f32),
        in_specs=[pl.BlockSpec(memory_space=pl.ANY)],
        out_specs=pl.BlockSpec(memory_space=pltpu.VMEM),
        scratch_shapes=[
            pltpu.VMEM((snap, depth), bf16),
            pltpu.VMEM((16, depth // PIECES), bf16),
            pltpu.VMEM((16, depth // PIECES), bf16),
            pltpu.VMEM((CHUNKS // 2, SLOT, 2 * width), bf16),
            pltpu.VMEM((LONG, BULK, width), bf16),
            pltpu.VMEM((LONG, BULK, width), bf16),
            pltpu.VMEM((HALF, BULK, width), bf16),
            pltpu.VMEM((GROUPS, CHIPS, 2, mine, TILE), f32),
            pltpu.VMEM((CHIPS, 2, mine, SLOT), f32),
            pltpu.VMEM((GROUPS, CHIPS, mine, TILE), f32),
            pltpu.VMEM((CHIPS, mine, SLOT), f32),
            pltpu.VMEM((GROUPS, 2, 4, mine, TILE), f32),
            pltpu.VMEM((CHIPS, mine, SLOT), f32),
            pltpu.VMEM((GROUPS, 4, 2, mine, TILE), f32),
            pltpu.VMEM((GROUPS, 2, mine, TILE), f32),
            pltpu.VMEM((GROUPS, mine, TILE), f32),
            pltpu.VMEM((4, mine, TILE), f32),
            pltpu.VMEM((4, mine, TILE), f32),
            pltpu.VMEM((CHIPS, mine, SLOT), f32),
            dma((GROUPS,)),
            dma((2,)),
            dma((CHUNKS,)),
            dma((CHUNKS,)),
            dma((2,)),
            dma((2, LONG)),
            dma((2, LONG)),
            dma((LONG,)),
            dma((2, HALF)),
            dma((HALF,)),
            dma((2, GROUPS)),
            dma((2, GROUPS, 4)),
            dma((2, GROUPS)),
            dma((2, CHIPS)),
        ],
        compiler_params=pltpu.CompilerParams(
            collective_id=0, has_side_effects=True, vmem_limit_bytes=56 * 2**20
        ),
        name="lagged_gram",
    )(snapshots)
    return summed[:, :columns] * (1.0 / total_rows)


def solution(mesh):
    return jax.shard_map(
        on_device,
        mesh=mesh,
        in_specs=(P("tm", "row"),),
        out_specs=P(("tm", "row"), None),
        check_vma=False,
    )
```
